32 devices in a mesh: dp: 16 (over z, x, core), mp: 2 (over y).
Axes of the slice: x: 2, y: 2, z: 4, core: 2. Of those that a mesh axis runs over, the one named last changes fastest.
Arguments:
- tokens: bfloat16 [6272, 512], P(('dp', 'mp')), may hold values from -6 to 6
- region_ids: int32 [32, 14, 14], P('dp'), may hold values from 0 to 3, as said below
- norm_gains: float32 [2, 2, 512], replicated, may hold values from 0.25 to 1.75
- norm_biases: float32 [2, 2, 512], replicated, may hold values from -2 to 2
- qkv_weight: bfloat16 [2, 512, 3, 512], P(None, 'dp', None, 'mp'), may hold values from -0.25 to 0.25
- qv_bias: float32 [2, 2, 512], P(None, None, 'mp'), may hold values from -3 to 3
- rel_table: float32 [2, 169, 16], P(None, None, 'mp'), may hold values from -4 to 4
- proj_weight: bfloat16 [2, 512, 512], P(None, 'mp', 'dp'), may hold values from -0.625 to 0.625
- proj_bias: float32 [2, 512], replicated, may hold values from -2 to 2
- fc1_weight: bfloat16 [2, 512, 2048], P(None, 'dp', 'mp'), may hold values from -0.25 to 0.25
- fc1_bias: float32 [2, 2048], P(None, 'mp'), may hold values from -3 to 3
- fc2_weight: bfloat16 [2, 2048, 512], P(None, 'mp', 'dp'), may hold values from -0.1875 to 0.1875
- fc2_bias: float32 [2, 512], replicated, may hold values from -2 to 2
- out_grad: bfloat16 [6272, 512], P(('dp', 'mp')), may hold values from -6 to 6
Outputs:
- block_out: bfloat16 [6272, 512], P(('dp', 'mp'))
- input_grad: bfloat16 [6272, 512], P(('dp', 'mp'))
- norm_gains_grad: float32 [2, 2, 512], replicated
- norm_biases_grad: float32 [2, 2, 512], replicated
- qkv_weight_grad: float32 [2, 512, 3, 512], P(None, 'dp', None, 'mp')
- qv_bias_grad: float32 [2, 2, 512], P(None, None, 'mp')
- rel_table_grad: float32 [2, 169, 16], P(None, None, 'mp')
- proj_weight_grad: float32 [2, 512, 512], P(None, 'mp', 'dp')
- proj_bias_grad: float32 [2, 512], replicated
- fc1_weight_grad: float32 [2, 512, 2048], P(None, 'dp', 'mp')
- fc1_bias_grad: float32 [2, 2048], P(None, 'mp')
- fc2_weight_grad: float32 [2, 2048, 512], P(None, 'mp', 'dp')
- fc2_bias_grad: float32 [2, 512], replicated
The draws below stay inside these ranges and needn't reach their ends.
Inputs may be any that keep to these rules, and one draw needn't show every extreme that they name: `region_ids`: for each image, ids of four rectangular crops: id = 2 * [row >= cut_row] + [column >= cut_col] with cuts of 1 to 13 drawn per image, so every image holds all four ids.
All inputs are finite; a program needn't handle non-finite values.
Results may differ from the reference program's by a relative error of at most 0.02.
Values may be sent and summed in bfloat16 or wider, within the bound.
A program may use at most 128 MiB of HBM per device.

```python
import functools
import math
import jax
import jax.numpy as jnp
from jax import lax

D = 512
HEADS = 16
HEAD_DIM = 32
FF = 2048
GRID = 14
WINDOW = 7
SHIFT = 3
LAYERS = 2
REL = 169
IMG_DEV = 2
IMAGES = 32
TOKENS = 6272
N_DP = 16


def draw_region_ids(key, part):
    key = jax.random.fold_in(key, 7)
    row_key, col_key = jax.random.split(key)
    row_cut = jax.random.randint(row_key, (IMAGES, 1, 1), 1, GRID)
    col_cut = jax.random.randint(col_key, (IMAGES, 1, 1), 1, GRID)
    places = jnp.arange(GRID, dtype=jnp.int32)
    lower = (places[None, :, None] >= row_cut).astype(jnp.int32)
    right = (places[None, None, :] >= col_cut).astype(jnp.int32)
    return (2 * lower + right).astype(jnp.int32)


def raised(values, rng, source, target, parts, factor):
    owner, partner = [(jnp.arange(values.shape[axis_at]) // (values.shape[axis_at] // parts)).reshape([-1 if axis == axis_at else 1 for axis in range(values.ndim)]) for axis_at in (source, target)]
    chosen = jax.random.permutation(rng, parts)[partner]
    strong = (owner == chosen) | (owner == (partner + parts // 2) % parts)
    return jnp.where(strong, factor * values, values)


def block_levels(own_key, extent, cuts, least, high):
    level = 1.0
    for position, parts in cuts:
        heights = jax.random.uniform(jax.random.fold_in(jax.random.fold_in(own_key, 6), position), (parts,), jnp.float32, least / len(cuts), high / len(cuts))
        level = level * jnp.repeat(jnp.exp(heights), extent[position] // parts).reshape((-1,) + (1,) * (len(extent) - 1 - position))
    return level


def bell_draw(own_key, dims, spread, limit, shards=(), held_as=jnp.bfloat16):
    values = spread * jax.random.normal(own_key, dims, jnp.float32)
    if shards:
        values = values * block_levels(own_key, dims, shards, -0.22, 0.18)
    return jnp.clip(values, -limit, limit).astype(held_as)


def gaussian_with(own_key, shape, deviation, limit, pieces, heavy, kind=jnp.bfloat16):
    array = deviation * jax.random.normal(own_key, shape, jnp.float32)
    if pieces:
        array = array * block_levels(own_key, shape, pieces, -0.22, 0.18)
    return jnp.clip(raised(array, jax.random.fold_in(own_key, 3), *heavy), -limit, limit).astype(kind)


def setup_inputs(seed: int = 0) -> dict:
    arg_keys = jax.random.split(jax.random.key(seed), 15)
    return {
        "tokens": gaussian_with(arg_keys[0], (TOKENS, D), 1.0, 6.0, ((0, 32),), (0, 1, 32, 2.75)),
        "region_ids": draw_region_ids(jax.random.fold_in(arg_keys[14], 71), 0),
        "norm_gains": jnp.clip(1.0 + 0.15 * jax.random.normal(arg_keys[2], (LAYERS, 2, D), jnp.float32), 0.25, 1.75),
        "norm_biases": bell_draw(arg_keys[3], (LAYERS, 2, D), 0.3, 2.0, (), jnp.float32),
        "qkv_weight": bell_draw(arg_keys[4], (LAYERS, D, 3, D), D ** -0.5, 0.25, ((1, 16), (3, 2))),
        "qv_bias": bell_draw(arg_keys[5], (LAYERS, 2, D), 0.5, 3.0, ((2, 2),), jnp.float32),
        "rel_table": bell_draw(arg_keys[6], (LAYERS, REL, HEADS), 1.0, 4.0, ((2, 2),), jnp.float32),
        "proj_weight": bell_draw(arg_keys[7], (LAYERS, D, D), (D // 6) ** -0.5, 0.625, ((1, 2), (2, 16))),
        "proj_bias": bell_draw(arg_keys[8], (LAYERS, D), 0.3, 2.0, (), jnp.float32),
        "fc1_weight": bell_draw(arg_keys[9], (LAYERS, D, FF), D ** -0.5, 0.25, ((1, 16), (2, 2))),
        "fc1_bias": bell_draw(arg_keys[10], (LAYERS, FF), 0.5, 3.0, ((1, 2),), jnp.float32),
        "fc2_weight": bell_draw(arg_keys[11], (LAYERS, FF, D), (FF // 2) ** -0.5, 0.1875, ((1, 2), (2, 16))),
        "fc2_bias": bell_draw(arg_keys[12], (LAYERS, D), 0.3, 2.0, (), jnp.float32),
        "out_grad": gaussian_with(arg_keys[13], (TOKENS, D), 1.0, 6.0, ((0, 32),), (0, 1, 32, 2.75)),
    }


@jax.custom_vjp
def low(v):
    return lax.optimization_barrier(v.astype(jnp.bfloat16)).astype(jnp.float32)

@jax.custom_vjp
def low_back(v):
    return v

def low_keep(v):
    return (low(v), None)

def low_pass(kept, grad):
    return (grad,)

def back_keep(v):
    return (v, None)

def back_low(kept, grad):
    return (low(grad),)
low.defvjp(low_keep, low_pass)
low_back.defvjp(back_keep, back_low)
highest = lax.Precision.HIGHEST
masked_score = -100.0
epsilon = 1e-05

def layer_norm(values, gain_row, offset_row):
    centred = values - lax.optimization_barrier(jnp.mean(values, axis=-1, keepdims=True))
    inverse = lax.rsqrt(lax.optimization_barrier(jnp.mean(centred * centred, axis=-1, keepdims=True)) + epsilon)
    return centred * inverse * gain_row + offset_row

def to_windows(rows, roll_by):
    images = rows.shape[0] // (GRID * GRID)
    width_all = rows.shape[1]
    grid_rows = rows.reshape(images, GRID, GRID, width_all)
    if roll_by:
        grid_rows = jnp.roll(grid_rows, (-roll_by, -roll_by), axis=(1, 2))
    blocks = GRID // WINDOW
    grid_rows = grid_rows.reshape(images, blocks, WINDOW, blocks, WINDOW, width_all).transpose(0, 1, 3, 2, 4, 5)
    return grid_rows.reshape(images * blocks * blocks, WINDOW * WINDOW, width_all)

def from_windows(windows, roll_by):
    blocks = GRID // WINDOW
    images = windows.shape[0] // (blocks * blocks)
    width_all = windows.shape[2]
    grid_rows = windows.reshape(images, blocks, blocks, WINDOW, WINDOW, width_all).transpose(0, 1, 3, 2, 4, 5)
    grid_rows = grid_rows.reshape(images, GRID, GRID, width_all)
    if roll_by:
        grid_rows = jnp.roll(grid_rows, (roll_by, roll_by), axis=(1, 2))
    return grid_rows.reshape(images * GRID * GRID, width_all)

def region_mask(region, roll_by):
    if roll_by:
        region = jnp.roll(region, (-roll_by, -roll_by), axis=(1, 2))
        places = jnp.arange(GRID, dtype=jnp.int32)
        band_id = (places >= GRID - WINDOW).astype(jnp.int32) + (places >= GRID - roll_by).astype(jnp.int32)
        region = region * 9 + band_id[None, :, None] * 3 + band_id[None, None, :]
    labels = to_windows(region.reshape(-1, 1), 0)[:, :, 0]
    return jnp.where(labels[:, :, None] == labels[:, None, :], 0.0, masked_score).astype(jnp.float32)

def position_index():
    places = jnp.arange(WINDOW * WINDOW, dtype=jnp.int32)
    row_of = places // WINDOW
    col_of = places % WINDOW
    return (row_of[:, None] - row_of[None, :] + WINDOW - 1) * (2 * WINDOW - 1) + (col_of[:, None] - col_of[None, :] + WINDOW - 1)

def swin_layer(state, region, params, depth):
    gains, offsets, qkv_mat, qv_add, table, proj_mat, proj_add, up_mat, up_add, down_mat, down_add = params
    roll_by = SHIFT if depth % 2 == 1 else 0
    normed = low(layer_norm(state, gains[depth, 0], offsets[depth, 0]))
    packed = jnp.einsum('rc,cte->rte', normed, qkv_mat[depth], precision=highest)
    bias_rows = jnp.stack([qv_add[depth, 0], jnp.zeros_like(qv_add[depth, 0]), qv_add[depth, 1]])
    packed = low(low_back(packed + bias_rows))
    windows = to_windows(packed.reshape(packed.shape[0], 3 * D), roll_by).reshape(-1, WINDOW * WINDOW, 3, HEADS, HEAD_DIM)
    relative = table[depth][position_index()].transpose(2, 0, 1)
    scores = jnp.einsum('wqhd,wkhd->whqk', windows[:, :, 0], windows[:, :, 1], precision=highest) * HEAD_DIM ** (-0.5)
    scores = low_back(scores + relative[None] + region_mask(region, roll_by)[:, None])
    chances = low(jax.nn.softmax(scores, axis=-1))
    mixed = jnp.einsum('whqk,wkhd->wqhd', chances, windows[:, :, 2], precision=highest)
    mixed = low(low_back(mixed))
    merged = from_windows(mixed.reshape(-1, WINDOW * WINDOW, D), roll_by)
    branch = low_back(jnp.dot(merged, proj_mat[depth], precision=highest) + proj_add[depth])
    middle = state + branch
    normed_two = low(layer_norm(middle, gains[depth, 1], offsets[depth, 1]))
    hidden = low_back(jnp.dot(normed_two, up_mat[depth], precision=highest) + up_add[depth])
    active = low(jax.nn.gelu(hidden, approximate=False))
    return middle + low_back(jnp.dot(active, down_mat[depth], precision=highest) + down_add[depth])

def forward(region, state, params):
    for depth in range(LAYERS):
        state = swin_layer(state, region, params, depth)
    return state

def reference(tokens, region_ids, norm_gains, norm_biases, qkv_weight, qv_bias, rel_table, proj_weight, proj_bias, fc1_weight, fc1_bias, fc2_weight, fc2_bias, out_grad):
    params = tuple((member.astype(jnp.float32) for member in (norm_gains, norm_biases, qkv_weight, qv_bias, rel_table, proj_weight, proj_bias, fc1_weight, fc1_bias, fc2_weight, fc2_bias)))
    per_block = IMG_DEV * math.gcd(N_DP, 4)
    block_count = IMAGES // per_block
    rows_block = per_block * GRID * GRID
    inputs = (tokens.reshape(block_count, rows_block, D), out_grad.reshape(block_count, rows_block, D), region_ids.reshape(block_count, per_block, GRID, GRID))

    def step_block(totals, inputs_block):
        block_in, block_grad, region = inputs_block
        result, pull = jax.vjp(functools.partial(forward, region), block_in.astype(jnp.float32), params)
        state_grad, weight_grads = pull(block_grad.astype(jnp.float32))
        totals = jax.tree.map(jnp.add, totals, weight_grads)
        return (totals, (result.astype(jnp.bfloat16), state_grad.astype(jnp.bfloat16)))
    zeros_all = jax.tree.map(jnp.zeros_like, params)
    totals, (outputs, state_grads) = lax.scan(step_block, zeros_all, inputs)
    return (outputs.reshape(TOKENS, D), state_grads.reshape(TOKENS, D), totals[0], totals[1], totals[2], totals[3], totals[4], totals[5], totals[6], totals[7], totals[8], totals[9], totals[10])
```

```python
import functools
import math

import jax
import jax.numpy as jnp
import numpy as np
from jax import lax
from jax.experimental import pallas as pl
from jax.experimental.pallas import tpu as pltpu
from jax.sharding import PartitionSpec as P

HEAD_DIM = 32
GRID = 14
WINDOW = 7
SHIFT = 3
REL = 169
AREA = WINDOW * WINDOW
SLOT = 64
ROWS = 256
WIDTH = 512
QKV = 768
HALF = 256
HID = 1024
COLS = QKV + HALF + HID + HID
HEADS = 16

masked_score = -100.0
blocked = -1e30
epsilon = 1e-05
root_half = 1.0 / math.sqrt(2.0)
inverse_root = 1.0 / math.sqrt(2.0 * math.pi)
scaling = HEAD_DIM ** (-0.5)
f32 = jnp.float32
bf16 = jnp.bfloat16


def dot_nn(a, b):
    return lax.dot_general(a, b, (((1,), (0,)), ((), ())), preferred_element_type=f32)


def dot_nt(a, b):
    return lax.dot_general(a, b, (((1,), (1,)), ((), ())), preferred_element_type=f32)


def dot_tn(a, b):
    return lax.dot_general(a, b, (((0,), (0,)), ((), ())), preferred_element_type=f32)


def token_places(roll_by):
    places = np.full((ROWS,), -1, np.int32)
    for window in range(4):
        for at in range(AREA):
            row = (window // 2) * WINDOW + at // WINDOW
            col = (window % 2) * WINDOW + at % WINDOW
            places[window * SLOT + at] = ((row + roll_by) % GRID) * GRID + (col + roll_by) % GRID
    return places


def permutation(roll_by):
    return (token_places(roll_by)[:, None] == np.arange(ROWS)[None, :]).astype(np.float32)


def permute(dot, perm, values):
    high = values.astype(bf16)
    rest = values - high.astype(f32)
    mid = rest.astype(bf16)
    low = (rest - mid.astype(f32)).astype(bf16)
    return (dot(perm, high) + dot(perm, mid)) + dot(perm, low)


def normalise(values):
    centred = values - jnp.mean(values, axis=-1, keepdims=True)
    inverse = lax.rsqrt(jnp.mean(centred * centred, axis=-1, keepdims=True) + epsilon)
    return centred * inverse, inverse


def norm_back(gradient, normed, inverse, gain_row):
    scaled = gradient * gain_row
    inner = (
        scaled
        - jnp.mean(scaled, axis=-1, keepdims=True)
        - normed * jnp.mean(scaled * normed, axis=-1, keepdims=True)
    )
    return (
        inner * inverse,
        jnp.sum(gradient * normed, axis=0, keepdims=True),
        jnp.sum(gradient, axis=0, keepdims=True),
    )


def weight(ref, half, start, width):
    return ref[:, half, :, start : start + width].reshape(WIDTH, width)


def lane_mask(head):
    lane = lax.broadcasted_iota(jnp.int32, (1, 128), 1)
    return jnp.where(lane // HEAD_DIM == head, 1.0, 0.0).astype(bf16)


def head_probs(query, key, rel_half, mask):
    relative = jnp.concatenate([rel_half, rel_half], axis=0)
    scores = dot_nt(query, key) * scaling + relative + mask
    raised = jnp.exp(scores - jnp.max(scores, axis=-1, keepdims=True))
    return raised / jnp.sum(raised, axis=-1, keepdims=True)


def forward_kernel(
    x_ref, perm_ref, w_ref, gain_ref, off_ref, qkvb_ref, rel_ref, mask_ref, projb_ref, upb_ref,
    downb_ref, out_ref, xw_ref, mid_ref, qkv_ref, mixed_ref, slope_ref, act_ref,
):
    perm = perm_ref[...]
    xw = permute(dot_nn, perm, x_ref[...])
    xw_ref[...] = xw
    normed = (normalise(xw)[0] * gain_ref[0:1, :] + off_ref[0:1, :]).astype(bf16)
    for m in range(2):
        packed = dot_nn(normed, weight(w_ref, m, 0, QKV)) + qkvb_ref[m : m + 1, :]
        qkv_ref[m] = packed.astype(bf16)

    def group(i, carry):
        m = i // 2
        lanes = pl.multiple_of((i % 2) * 128, 128)
        for p in range(2):
            rows = slice(p * 128, p * 128 + 128)
            query = qkv_ref[m, rows, pl.ds(lanes, 128)]
            key = qkv_ref[m, rows, pl.ds(lanes + HALF, 128)]
            value = qkv_ref[m, rows, pl.ds(lanes + 2 * HALF, 128)]
            total = jnp.zeros((128, 128), f32)
            for h in range(4):
                sel = lane_mask(h)
                probs = head_probs(query * sel, key, rel_ref[i * 4 + h], mask_ref[p])
                total = total + dot_nn(probs.astype(bf16), value * sel)
            mixed_ref[m, rows, pl.ds(lanes, 128)] = total.astype(bf16)
        return carry

    lax.fori_loop(0, 4, group, 0)
    mid = xw + (
        dot_nt(mixed_ref[0], weight(w_ref, 0, QKV, HALF))
        + dot_nt(mixed_ref[1], weight(w_ref, 1, QKV, HALF))
        + projb_ref[...]
    )
    mid_ref[...] = mid
    normed = (normalise(mid)[0] * gain_ref[1:2, :] + off_ref[1:2, :]).astype(bf16)
    branch = jnp.zeros((ROWS, WIDTH), f32)
    for m in range(2):
        pre = dot_nn(normed, weight(w_ref, m, QKV + HALF, HID)) + upb_ref[m : m + 1, :]
        cdf = 0.5 * (1.0 + lax.erf(pre * root_half))
        active = (pre * cdf).astype(bf16)
        slope_ref[m] = cdf + pre * jnp.exp(-0.5 * pre * pre) * inverse_root
        act_ref[m] = active
        branch = branch + dot_nt(active, weight(w_ref, m, QKV + HALF + HID, HID))
    out_ref[...] = permute(dot_tn, perm, mid + (branch + downb_ref[...]))


def backward_kernel(
    g_ref, perm_ref, w_ref, gain_ref, off_ref, rel_ref, mask_ref, xw_ref, mid_ref, qkv_ref,
    mixed_ref, slope_ref, act_ref,
    out_ref, wg_ref, gaing_ref, offg_ref, qkvbg_ref, projbg_ref, upbg_ref, downbg_ref, relg_ref,
    dmix_ref, dqkv_ref,
):
    def put(m, start, width, value):
        wg_ref[:, m, :, start : start + width] = value.astype(bf16).reshape(16, 32, width)

    perm = perm_ref[...]
    grad = permute(dot_nn, perm, g_ref[...])
    mlp_grad = grad.astype(bf16)
    downbg_ref[...] = jnp.sum(mlp_grad.astype(f32), axis=0, keepdims=True)
    hat, inverse = normalise(mid_ref[...])
    normed = (hat * gain_ref[1:2, :] + off_ref[1:2, :]).astype(bf16)
    norm_grad = jnp.zeros((ROWS, WIDTH), f32)
    for m in range(2):
        act_grad = dot_nn(mlp_grad, weight(w_ref, m, QKV + HALF + HID, HID))
        pre_grad = (act_grad * slope_ref[m]).astype(bf16)
        upbg_ref[m : m + 1, :] = jnp.sum(pre_grad.astype(f32), axis=0, keepdims=True)
        put(m, QKV + HALF + HID, HID, dot_tn(mlp_grad, act_ref[m]))
        put(m, QKV + HALF, HID, dot_tn(normed, pre_grad))
        norm_grad = norm_grad + dot_nt(pre_grad, weight(w_ref, m, QKV + HALF, HID))
    back, gain_sum, off_sum = norm_back(norm_grad, hat, inverse, gain_ref[1:2, :])
    gaing_ref[1:2, :] = gain_sum
    offg_ref[1:2, :] = off_sum
    grad = grad + back
    attn_grad = grad.astype(bf16)
    projbg_ref[...] = jnp.sum(attn_grad.astype(f32), axis=0, keepdims=True)
    for m in range(2):
        put(m, QKV, HALF, dot_tn(attn_grad, mixed_ref[m]))
        dmix_ref[m] = dot_nn(attn_grad, weight(w_ref, m, QKV, HALF)).astype(bf16)

    def group(i, carry):
        m = i // 2
        lanes = pl.multiple_of((i % 2) * 128, 128)
        for h in range(4):
            relg_ref[i * 4 + h] = jnp.zeros((128, 128), f32)
        for p in range(2):
            rows = slice(p * 128, p * 128 + 128)
            query = qkv_ref[m, rows, pl.ds(lanes, 128)]
            key = qkv_ref[m, rows, pl.ds(lanes + HALF, 128)]
            value = qkv_ref[m, rows, pl.ds(lanes + 2 * HALF, 128)]
            dmix = dmix_ref[m, rows, pl.ds(lanes, 128)]
            dquery = jnp.zeros((128, 128), f32)
            dkey = jnp.zeros((128, 128), f32)
            dvalue = jnp.zeros((128, 128), f32)
            for h in range(4):
                sel = lane_mask(h)
                query_h = query * sel
                dmix_h = dmix * sel
                probs = head_probs(query_h, key, rel_ref[i * 4 + h], mask_ref[p])
                dvalue = dvalue + dot_tn(probs.astype(bf16), dmix_h)
                dprobs = dot_nt(dmix_h, value)
                dscore = (
                    probs * (dprobs - jnp.sum(probs * dprobs, axis=-1, keepdims=True))
                ).astype(bf16)
                relg_ref[i * 4 + h] += dscore.astype(f32)
                dquery = dquery + dot_nn(dscore, key * sel)
                dkey = dkey + dot_tn(dscore, query_h)
            dqkv_ref[m, rows, pl.ds(lanes, 128)] = (dquery * scaling).astype(bf16)
            dqkv_ref[m, rows, pl.ds(lanes + HALF, 128)] = (dkey * scaling).astype(bf16)
            dqkv_ref[m, rows, pl.ds(lanes + 2 * HALF, 128)] = dvalue.astype(bf16)
        return carry

    lax.fori_loop(0, 4, group, 0)
    hat, inverse = normalise(xw_ref[...])
    normed = (hat * gain_ref[0:1, :] + off_ref[0:1, :]).astype(bf16)
    norm_grad = jnp.zeros((ROWS, WIDTH), f32)
    for m in range(2):
        dqkv = dqkv_ref[m]
        qkvbg_ref[m : m + 1, :] = jnp.sum(dqkv.astype(f32), axis=0, keepdims=True)
        put(m, 0, QKV, dot_tn(normed, dqkv))
        norm_grad = norm_grad + dot_nt(dqkv, weight(w_ref, m, 0, QKV))
    back, gain_sum, off_sum = norm_back(norm_grad, hat, inverse, gain_ref[0:1, :])
    gaing_ref[0:1, :] = gain_sum
    offg_ref[0:1, :] = off_sum
    out_ref[...] = permute(dot_tn, perm, grad + back)


def whole(shape):
    return pl.BlockSpec(shape, lambda i: (0,) * len(shape), pipeline_mode=pl.Buffered(1))


def call_kernel(body, depth, operands, outs, scratch, flops):
    specs = [
        pl.BlockSpec(
            (16, 2, 32, COLS), lambda i: (0, 0, 0, depth), pipeline_mode=pl.Buffered(1)
        )
        if position == 2
        else whole(member.shape)
        for position, member in enumerate(operands)
    ]
    return pl.pallas_call(
        body,
        grid=(1,),
        out_shape=[jax.ShapeDtypeStruct(shape, kind) for shape, kind in outs],
        in_specs=specs,
        out_specs=[whole(shape) for shape, _ in outs],
        scratch_shapes=scratch,
        compiler_params=pltpu.CompilerParams(vmem_limit_bytes=56 * 1024 * 1024),
        cost_estimate=pl.CostEstimate(
            flops=flops, bytes_accessed=20_000_000, transcendentals=2_000_000
        ),
    )(*operands)


def pair_masks(region, roll_by):
    places = token_places(roll_by)
    valid = places >= 0
    labels = region.reshape(-1)[jnp.asarray(np.where(valid, places, 0))]
    if roll_by:
        band = np.zeros((ROWS,), np.int32)
        for window in range(4):
            for at in range(AREA):
                row = (window // 2) * WINDOW + at // WINDOW
                col = (window % 2) * WINDOW + at % WINDOW
                ids = [int(v >= GRID - WINDOW) + int(v >= GRID - roll_by) for v in (row, col)]
                band[window * SLOT + at] = 3 * ids[0] + ids[1]
        labels = labels * 9 + jnp.asarray(band)
    labels = labels.reshape(2, 128)
    window_of = (np.arange(ROWS) // SLOT).reshape(2, 128)
    usable = (window_of[:, :, None] == window_of[:, None, :]) & valid.reshape(2, 1, 128)
    same = labels[:, :, None] == labels[:, None, :]
    return jnp.where(jnp.asarray(usable), jnp.where(same, 0.0, masked_score), blocked).astype(f32)


def pair_index():
    places = np.arange(SLOT)
    row_of, col_of = places // WINDOW, places % WINDOW
    index = (row_of[:, None] - row_of[None, :] + WINDOW - 1) * (2 * WINDOW - 1) + (
        col_of[:, None] - col_of[None, :] + WINDOW - 1
    )
    inside = (places[:, None] < AREA) & (places[None, :] < AREA)
    return np.where(inside, index, -1)


def per_device(
    tokens,
    region_ids,
    norm_gains,
    norm_biases,
    qkv_weight,
    qv_bias,
    rel_table,
    proj_weight,
    proj_bias,
    fc1_weight,
    fc1_bias,
    fc2_weight,
    fc2_bias,
    out_grad,
):
    layer_total = qkv_weight.shape[0]
    n_dp = lax.axis_size("dp")
    devices = n_dp * 2
    both = ("dp", "mp")
    mp_index = lax.axis_index("mp")
    shard_rows = qkv_weight.shape[1]
    count = tokens.shape[0]

    parts = []
    for depth in range(layer_total):
        parts += [
            qkv_weight[depth].reshape(shard_rows, QKV),
            proj_weight[depth].T,
            fc1_weight[depth],
            fc2_weight[depth].T,
        ]
    shard = jnp.concatenate(parts, axis=1)
    weights = lax.all_gather(shard, both, axis=0, tiled=True)
    weights = weights.reshape(n_dp, 2, shard_rows, layer_total * COLS)
    if n_dp != 16:
        weights = weights.transpose(1, 0, 2, 3).reshape(2, 16, 32, layer_total * COLS)
        weights = weights.transpose(1, 0, 2, 3)

    small = jnp.concatenate([qv_bias.reshape(-1), rel_table.reshape(-1), fc1_bias.reshape(-1)])
    other = lax.ppermute(small, "mp", [(0, 1), (1, 0)])
    lower = mp_index == 0
    small = jnp.stack([jnp.where(lower, small, other), jnp.where(lower, other, small)])
    first, second = qv_bias.size, qv_bias.size + rel_table.size
    qv_all = small[:, :first].reshape(2, layer_total, 2, HALF)
    rel_all = small[:, first:second].reshape(2, layer_total, REL, HEADS // 2)
    up_all = small[:, second:].reshape(2, layer_total, HID)

    index = pair_index().reshape(-1)
    hot = jnp.asarray((index[:, None] == np.arange(REL)[None, :]).astype(np.float32)).astype(bf16)
    table = rel_all.transpose(1, 0, 3, 2).reshape(layer_total * HEADS, REL)

    def exact_dot(left, right, dims):
        high = left.astype(bf16)
        rest = left - high.astype(f32)
        mid = rest.astype(bf16)
        low = (rest - mid.astype(f32)).astype(bf16)
        stacked = jnp.concatenate([high, mid, low], axis=0)
        product = lax.dot_general(stacked, right, dims, preferred_element_type=f32)
        product = product.reshape((3,) + (left.shape[0],) + product.shape[1:])
        return (product[0] + product[1]) + product[2]

    relative = exact_dot(table, hot, (((1,), (1,)), ((), ())))
    relative = relative.reshape(layer_total, HEADS, SLOT, SLOT)
    relative = jnp.concatenate([relative, relative], axis=3)

    region = lax.dynamic_index_in_dim(region_ids, mp_index, 0, keepdims=False)
    rolls = [SHIFT if depth % 2 == 1 else 0 for depth in range(layer_total)]
    perms = {roll: jnp.asarray(permutation(roll)).astype(bf16) for roll in (0, SHIFT)}
    masks = {roll: pair_masks(region, roll) for roll in (0, SHIFT)}

    state = jnp.pad(tokens.astype(f32), ((0, ROWS - count), (0, 0)))
    records = []
    for depth in range(layer_total):
        roll = rolls[depth]
        bias = jnp.concatenate(
            [qv_all[:, depth, 0], jnp.zeros((2, HALF), f32), qv_all[:, depth, 1]], axis=1
        )
        operands = (
            state, perms[roll], weights, norm_gains[depth], norm_biases[depth], bias,
            relative[depth], masks[roll], proj_bias[depth][None], up_all[:, depth],
            fc2_bias[depth][None],
        )
        outs = (
            ((ROWS, WIDTH), f32), ((ROWS, WIDTH), f32), ((ROWS, WIDTH), f32),
            ((2, ROWS, QKV), bf16), ((2, ROWS, HALF), bf16),
            ((2, ROWS, HID), f32), ((2, ROWS, HID), bf16),
        )
        state, *saved = call_kernel(forward_kernel, depth, operands, outs, [], 2_000_000_000)
        records.append(saved)
    block_out = state[:count].astype(bf16)

    gradient = jnp.pad(out_grad.astype(f32), ((0, ROWS - count), (0, 0)))
    totals = [None] * layer_total
    small_rows = [None] * layer_total
    for depth in reversed(range(layer_total)):
        roll = rolls[depth]
        operands = (
            gradient, perms[roll], weights, norm_gains[depth], norm_biases[depth],
            relative[depth], masks[roll], *records[depth],
        )
        outs = (
            ((ROWS, WIDTH), f32), ((16, 2, 32, COLS), bf16), ((2, WIDTH), f32), ((2, WIDTH), f32),
            ((2, QKV), f32), ((1, WIDTH), f32), ((2, HID), f32), ((1, WIDTH), f32),
            ((HEADS, 128, 128), f32),
        )
        scratch = [pltpu.VMEM((2, ROWS, HALF), bf16), pltpu.VMEM((2, ROWS, QKV), bf16)]
        gradient, wide, *rest = call_kernel(
            backward_kernel, depth, operands, outs, scratch, 4_000_000_000
        )
        if n_dp != 16:
            wide = wide.transpose(1, 0, 2, 3).reshape(2, n_dp, shard_rows, COLS)
            wide = wide.transpose(1, 0, 2, 3)
        wide = wide.reshape(devices * shard_rows, COLS)
        owned = lax.psum_scatter(wide, both, scatter_dimension=0, tiled=True)
        totals[depth] = owned.astype(f32)
        gain_sum, off_sum, qkvb_sum, projb_sum, upb_sum, downb_sum, rel_sum = rest
        pairs = rel_sum[:, :SLOT, :SLOT] + rel_sum[:, SLOT:, SLOT:]
        qv_sum = jnp.stack([qkvb_sum[:, :HALF], qkvb_sum[:, 2 * HALF :]]).reshape(-1)
        small_rows[depth] = (gain_sum, off_sum, qv_sum, projb_sum, upb_sum, downb_sum, pairs)

    pairs = jnp.concatenate([row[6].reshape(HEADS, -1) for row in small_rows], axis=0)
    table_sum = exact_dot(pairs, hot, (((1,), (0,)), ((), ())))
    member = jnp.concatenate(
        [jnp.concatenate([piece.reshape(-1) for piece in row[:6]]) for row in small_rows]
        + [table_sum.reshape(-1)]
    )
    extent = member.size
    padded = -(-extent // (devices * 128)) * devices * 128
    member = jnp.pad(member, (0, padded - extent)).reshape(devices, padded // devices)
    own = jnp.sum(lax.all_to_all(member, both, 0, 0), axis=0)
    summed = lax.all_gather(own, both, axis=0, tiled=True)
    each = (extent - table_sum.size) // layer_total
    rows = summed[: each * layer_total].reshape(layer_total, each)
    sizes = (2 * WIDTH, 2 * WIDTH, 4 * HALF, WIDTH, 2 * HID, WIDTH)
    edges = np.concatenate([[0], np.cumsum(sizes)])
    gain_t, off_t, qv_t, projb_t, upb_t, downb_t = [
        rows[:, edges[k] : edges[k + 1]] for k in range(6)
    ]
    table_t = summed[each * layer_total : extent].reshape(layer_total, 2, HEADS // 2, REL)
    pick = lambda array, axis: lax.dynamic_index_in_dim(array, mp_index, axis, keepdims=False)
    stacked = jnp.stack(totals)
    ends = np.concatenate([[0], np.cumsum((QKV, HALF, HID, HID))])
    qkv_t, proj_t, up_t, down_t = [stacked[:, :, ends[k] : ends[k + 1]] for k in range(4)]
    return (
        block_out,
        gradient[:count].astype(bf16),
        gain_t.reshape(layer_total, 2, WIDTH),
        off_t.reshape(layer_total, 2, WIDTH),
        qkv_t.reshape(layer_total, shard_rows, 3, HALF),
        pick(qv_t.reshape(layer_total, 2, 2, HALF), 2),
        pick(table_t, 1).transpose(0, 2, 1),
        proj_t.transpose(0, 2, 1),
        projb_t,
        up_t,
        pick(upb_t.reshape(layer_total, 2, HID), 1),
        down_t.transpose(0, 2, 1),
        downb_t,
    )


def solution(mesh):
    in_specs = (
        P(("dp", "mp"), None),
        P("dp", None, None),
        P(),
        P(),
        P(None, "dp", None, "mp"),
        P(None, None, "mp"),
        P(None, None, "mp"),
        P(None, "mp", "dp"),
        P(),
        P(None, "dp", "mp"),
        P(None, "mp"),
        P(None, "mp", "dp"),
        P(),
        P(("dp", "mp"), None),
    )
    out_specs = (
        P(("dp", "mp"), None),
        P(("dp", "mp"), None),
        P(),
        P(),
        P(None, "dp", None, "mp"),
        P(None, None, "mp"),
        P(None, None, "mp"),
        P(None, "mp", "dp"),
        P(),
        P(None, "dp", "mp"),
        P(None, "mp"),
        P(None, "mp", "dp"),
        P(),
    )
    return jax.shard_map(
        per_device, mesh=mesh, in_specs=in_specs, out_specs=out_specs, check_vma=False
    )
```

```python
import functools
import math

import jax
import jax.numpy as jnp
import numpy as np
from jax import lax
from jax.experimental import pallas as pl
from jax.experimental.pallas import tpu as pltpu
from jax.sharding import PartitionSpec as P

HEAD_DIM = 32
GRID = 14
WINDOW = 7
SHIFT = 3
REL = 169
AREA = WINDOW * WINDOW
SLOT = 64
ROWS = 256
WIDTH = 512
QKV = 768
HALF = 256
HID = 1024
COLS = QKV + HALF + HID + HID
HEADS = 16

masked_score = -100.0
blocked = -1e30
epsilon = 1e-05
root_half = 1.0 / math.sqrt(2.0)
inverse_root = 1.0 / math.sqrt(2.0 * math.pi)
scaling = HEAD_DIM ** (-0.5)
f32 = jnp.float32
bf16 = jnp.bfloat16


def dot_nn(a, b):
    return lax.dot_general(a, b, (((1,), (0,)), ((), ())), preferred_element_type=f32)


def dot_nt(a, b):
    return lax.dot_general(a, b, (((1,), (1,)), ((), ())), preferred_element_type=f32)


def dot_tn(a, b):
    return lax.dot_general(a, b, (((0,), (0,)), ((), ())), preferred_element_type=f32)


def token_places(roll_by):
    places = np.full((ROWS,), -1, np.int32)
    for window in range(4):
        for at in range(AREA):
            row = (window // 2) * WINDOW + at // WINDOW
            col = (window % 2) * WINDOW + at % WINDOW
            places[window * SLOT + at] = ((row + roll_by) % GRID) * GRID + (col + roll_by) % GRID
    return places


def permutation(roll_by):
    return (token_places(roll_by)[:, None] == np.arange(ROWS)[None, :]).astype(np.float32)


def permute(dot, perm, values):
    high = values.astype(bf16)
    rest = values - high.astype(f32)
    mid = rest.astype(bf16)
    low = (rest - mid.astype(f32)).astype(bf16)
    return (dot(perm, high) + dot(perm, mid)) + dot(perm, low)


def normalise(values):
    centred = values - jnp.mean(values, axis=-1, keepdims=True)
    inverse = lax.rsqrt(jnp.mean(centred * centred, axis=-1, keepdims=True) + epsilon)
    return centred * inverse, inverse


def norm_back(gradient, normed, inverse, gain_row):
    scaled = gradient * gain_row
    inner = (
        scaled
        - jnp.mean(scaled, axis=-1, keepdims=True)
        - normed * jnp.mean(scaled * normed, axis=-1, keepdims=True)
    )
    return (
        inner * inverse,
        jnp.sum(gradient * normed, axis=0, keepdims=True),
        jnp.sum(gradient, axis=0, keepdims=True),
    )


def weight(ref, half, start, width):
    return ref[:, half, :, start : start + width].reshape(WIDTH, width)


def lane_mask(head):
    lane = lax.broadcasted_iota(jnp.int32, (1, 128), 1)
    return jnp.where(lane // HEAD_DIM == head, 1.0, 0.0).astype(bf16)


def head_probs(query, key, rel_half, mask):
    relative = jnp.concatenate([rel_half, rel_half], axis=0)
    scores = dot_nt(query, key) * scaling + relative + mask
    raised = jnp.exp(scores - jnp.max(scores, axis=-1, keepdims=True))
    return raised / jnp.sum(raised, axis=-1, keepdims=True)


def forward_kernel(
    x_ref, perm_ref, w_ref, gain_ref, off_ref, qkvb_ref, rel_ref, mask_ref, projb_ref, upb_ref,
    downb_ref, out_ref, xw_ref, mid_ref, qkv_ref, mixed_ref, slope_ref, act_ref,
):
    perm = perm_ref[...]
    xw = permute(dot_nn, perm, x_ref[...])
    xw_ref[...] = xw
    normed = (normalise(xw)[0] * gain_ref[0:1, :] + off_ref[0:1, :]).astype(bf16)
    for m in range(2):
        packed = dot_nn(normed, weight(w_ref, m, 0, QKV)) + qkvb_ref[m : m + 1, :]
        qkv_ref[m] = packed.astype(bf16)

    def group(i, carry):
        m = i // 2
        lanes = pl.multiple_of((i % 2) * 128, 128)
        for p in range(2):
            rows = slice(p * 128, p * 128 + 128)
            query = qkv_ref[m, rows, pl.ds(lanes, 128)]
            key = qkv_ref[m, rows, pl.ds(lanes + HALF, 128)]
            value = qkv_ref[m, rows, pl.ds(lanes + 2 * HALF, 128)]
            total = jnp.zeros((128, 128), f32)
            for h in range(4):
                sel = lane_mask(h)
                probs = head_probs(query * sel, key, rel_ref[i * 4 + h], mask_ref[p])
                total = total + dot_nn(probs.astype(bf16), value * sel)
            mixed_ref[m, rows, pl.ds(lanes, 128)] = total.astype(bf16)
        return carry

    lax.fori_loop(0, 4, group, 0)
    mid = xw + (
        dot_nt(mixed_ref[0], weight(w_ref, 0, QKV, HALF))
        + dot_nt(mixed_ref[1], weight(w_ref, 1, QKV, HALF))
        + projb_ref[...]
    )
    mid_ref[...] = mid
    normed = (normalise(mid)[0] * gain_ref[1:2, :] + off_ref[1:2, :]).astype(bf16)
    branch = jnp.zeros((ROWS, WIDTH), f32)
    for m in range(2):
        pre = dot_nn(normed, weight(w_ref, m, QKV + HALF, HID)) + upb_ref[m : m + 1, :]
        cdf = 0.5 * (1.0 + lax.erf(pre * root_half))
        active = (pre * cdf).astype(bf16)
        slope_ref[m] = cdf + pre * jnp.exp(-0.5 * pre * pre) * inverse_root
        act_ref[m] = active
        branch = branch + dot_nt(active, weight(w_ref, m, QKV + HALF + HID, HID))
    out_ref[...] = permute(dot_tn, perm, mid + (branch + downb_ref[...]))


def backward_kernel(
    g_ref, perm_ref, w_ref, gain_ref, off_ref, rel_ref, mask_ref, xw_ref, mid_ref, qkv_ref,
    mixed_ref, slope_ref, act_ref,
    out_ref, wg_ref, gaing_ref, offg_ref, qkvbg_ref, projbg_ref, upbg_ref, downbg_ref, relg_ref,
    dmix_ref, dqkv_ref,
):
    def put(m, start, width, value):
        wg_ref[:, m, :, start : start + width] = value.astype(bf16).reshape(16, 32, width)

    perm = perm_ref[...]
    grad = permute(dot_nn, perm, g_ref[...])
    mlp_grad = grad.astype(bf16)
    downbg_ref[...] = jnp.sum(mlp_grad.astype(f32), axis=0, keepdims=True)
    hat, inverse = normalise(mid_ref[...])
    normed = (hat * gain_ref[1:2, :] + off_ref[1:2, :]).astype(bf16)
    norm_grad = jnp.zeros((ROWS, WIDTH), f32)
    for m in range(2):
        act_grad = dot_nn(mlp_grad, weight(w_ref, m, QKV + HALF + HID, HID))
        pre_grad = (act_grad * slope_ref[m]).astype(bf16)
        upbg_ref[m : m + 1, :] = jnp.sum(pre_grad.astype(f32), axis=0, keepdims=True)
        put(m, QKV + HALF + HID, HID, dot_tn(mlp_grad, act_ref[m]))
        put(m, QKV + HALF, HID, dot_tn(normed, pre_grad))
        norm_grad = norm_grad + dot_nt(pre_grad, weight(w_ref, m, QKV + HALF, HID))
    back, gain_sum, off_sum = norm_back(norm_grad, hat, inverse, gain_ref[1:2, :])
    gaing_ref[1:2, :] = gain_sum
    offg_ref[1:2, :] = off_sum
    grad = grad + back
    attn_grad = grad.astype(bf16)
    projbg_ref[...] = jnp.sum(attn_grad.astype(f32), axis=0, keepdims=True)
    for m in range(2):
        put(m, QKV, HALF, dot_tn(attn_grad, mixed_ref[m]))
        dmix_ref[m] = dot_nn(attn_grad, weight(w_ref, m, QKV, HALF)).astype(bf16)

    def group(i, carry):
        m = i // 2
        lanes = pl.multiple_of((i % 2) * 128, 128)
        for h in range(4):
            relg_ref[i * 4 + h] = jnp.zeros((128, 128), f32)
        for p in range(2):
            rows = slice(p * 128, p * 128 + 128)
            query = qkv_ref[m, rows, pl.ds(lanes, 128)]
            key = qkv_ref[m, rows, pl.ds(lanes + HALF, 128)]
            value = qkv_ref[m, rows, pl.ds(lanes + 2 * HALF, 128)]
            dmix = dmix_ref[m, rows, pl.ds(lanes, 128)]
            dquery = jnp.zeros((128, 128), f32)
            dkey = jnp.zeros((128, 128), f32)
            dvalue = jnp.zeros((128, 128), f32)
            for h in range(4):
                sel = lane_mask(h)
                query_h = query * sel
                dmix_h = dmix * sel
                probs = head_probs(query_h, key, rel_ref[i * 4 + h], mask_ref[p])
                dvalue = dvalue + dot_tn(probs.astype(bf16), dmix_h)
                dprobs = dot_nt(dmix_h, value)
                dscore = (
                    probs * (dprobs - jnp.sum(probs * dprobs, axis=-1, keepdims=True))
                ).astype(bf16)
                relg_ref[i * 4 + h] += dscore.astype(f32)
                dquery = dquery + dot_nn(dscore, key * sel)
                dkey = dkey + dot_tn(dscore, query_h)
            dqkv_ref[m, rows, pl.ds(lanes, 128)] = (dquery * scaling).astype(bf16)
            dqkv_ref[m, rows, pl.ds(lanes + HALF, 128)] = (dkey * scaling).astype(bf16)
            dqkv_ref[m, rows, pl.ds(lanes + 2 * HALF, 128)] = dvalue.astype(bf16)
        return carry

    lax.fori_loop(0, 4, group, 0)
    hat, inverse = normalise(xw_ref[...])
    normed = (hat * gain_ref[0:1, :] + off_ref[0:1, :]).astype(bf16)
    norm_grad = jnp.zeros((ROWS, WIDTH), f32)
    for m in range(2):
        dqkv = dqkv_ref[m]
        qkvbg_ref[m : m + 1, :] = jnp.sum(dqkv.astype(f32), axis=0, keepdims=True)
        put(m, 0, QKV, dot_tn(normed, dqkv))
        norm_grad = norm_grad + dot_nt(dqkv, weight(w_ref, m, 0, QKV))
    back, gain_sum, off_sum = norm_back(norm_grad, hat, inverse, gain_ref[0:1, :])
    gaing_ref[0:1, :] = gain_sum
    offg_ref[0:1, :] = off_sum
    out_ref[...] = permute(dot_tn, perm, grad + back)


def whole(shape):
    return pl.BlockSpec(shape, lambda i: (0,) * len(shape), pipeline_mode=pl.Buffered(1))


def call_kernel(body, depth, operands, outs, scratch, flops, wide_at=None, shared=None):
    specs = [
        pl.BlockSpec(
            (16, 2, 32, COLS), lambda i: (0, 0, 0, depth), pipeline_mode=pl.Buffered(1)
        )
        if position == 2
        else whole(member.shape)
        for position, member in enumerate(operands)
    ]
    out_specs = [whole(shape) for shape, _ in outs]
    aliases = {}
    if wide_at is not None:
        out_specs[wide_at] = pl.BlockSpec(
            (16, 2, 32, COLS), lambda i: (0, 0, 0, depth), pipeline_mode=pl.Buffered(1)
        )
    if shared is not None:
        aliases = {len(operands): wide_at}
        operands = tuple(operands) + (shared,)
        specs.append(pl.BlockSpec(memory_space=pl.ANY))
        plain, taken = body, len(operands) - 1
        body = lambda *refs: plain(*refs[:taken], *refs[taken + 1 :])
    return pl.pallas_call(
        body,
        grid=(1,),
        out_shape=[jax.ShapeDtypeStruct(shape, kind) for shape, kind in outs],
        in_specs=specs,
        out_specs=out_specs,
        input_output_aliases=aliases,
        scratch_shapes=scratch,
        compiler_params=pltpu.CompilerParams(vmem_limit_bytes=56 * 1024 * 1024),
        cost_estimate=pl.CostEstimate(
            flops=flops, bytes_accessed=20_000_000, transcendentals=2_000_000
        ),
    )(*operands)


def pair_masks(region, roll_by):
    places = token_places(roll_by)
    valid = places >= 0
    labels = region.reshape(-1)[jnp.asarray(np.where(valid, places, 0))]
    if roll_by:
        band = np.zeros((ROWS,), np.int32)
        for window in range(4):
            for at in range(AREA):
                row = (window // 2) * WINDOW + at // WINDOW
                col = (window % 2) * WINDOW + at % WINDOW
                ids = [int(v >= GRID - WINDOW) + int(v >= GRID - roll_by) for v in (row, col)]
                band[window * SLOT + at] = 3 * ids[0] + ids[1]
        labels = labels * 9 + jnp.asarray(band)
    labels = labels.reshape(2, 128)
    window_of = (np.arange(ROWS) // SLOT).reshape(2, 128)
    usable = (window_of[:, :, None] == window_of[:, None, :]) & valid.reshape(2, 1, 128)
    same = labels[:, :, None] == labels[:, None, :]
    return jnp.where(jnp.asarray(usable), jnp.where(same, 0.0, masked_score), blocked).astype(f32)


def pair_index():
    places = np.arange(SLOT)
    row_of, col_of = places // WINDOW, places % WINDOW
    index = (row_of[:, None] - row_of[None, :] + WINDOW - 1) * (2 * WINDOW - 1) + (
        col_of[:, None] - col_of[None, :] + WINDOW - 1
    )
    inside = (places[:, None] < AREA) & (places[None, :] < AREA)
    return np.where(inside, index, -1)


def per_device(
    tokens,
    region_ids,
    norm_gains,
    norm_biases,
    qkv_weight,
    qv_bias,
    rel_table,
    proj_weight,
    proj_bias,
    fc1_weight,
    fc1_bias,
    fc2_weight,
    fc2_bias,
    out_grad,
):
    layer_total = qkv_weight.shape[0]
    n_dp = lax.axis_size("dp")
    devices = n_dp * 2
    both = ("dp", "mp")
    mp_index = lax.axis_index("mp")
    shard_rows = qkv_weight.shape[1]
    count = tokens.shape[0]

    parts = []
    for depth in range(layer_total):
        parts += [
            qkv_weight[depth].reshape(shard_rows, QKV),
            proj_weight[depth].T,
            fc1_weight[depth],
            fc2_weight[depth].T,
        ]
    shard = jnp.concatenate(parts, axis=1)
    weights = lax.all_gather(shard, both, axis=0, tiled=True)
    weights = weights.reshape(n_dp, 2, shard_rows, layer_total * COLS)
    if n_dp != 16:
        weights = weights.transpose(1, 0, 2, 3).reshape(2, 16, 32, layer_total * COLS)
        weights = weights.transpose(1, 0, 2, 3)

    small = jnp.concatenate([qv_bias.reshape(-1), rel_table.reshape(-1), fc1_bias.reshape(-1)])
    other = lax.ppermute(small, "mp", [(0, 1), (1, 0)])
    lower = mp_index == 0
    small = jnp.stack([jnp.where(lower, small, other), jnp.where(lower, other, small)])
    first, second = qv_bias.size, qv_bias.size + rel_table.size
    qv_all = small[:, :first].reshape(2, layer_total, 2, HALF)
    rel_all = small[:, first:second].reshape(2, layer_total, REL, HEADS // 2)
    up_all = small[:, second:].reshape(2, layer_total, HID)

    index = pair_index().reshape(-1)
    hot = jnp.asarray((index[:, None] == np.arange(REL)[None, :]).astype(np.float32)).astype(bf16)
    table = rel_all.transpose(1, 0, 3, 2).reshape(layer_total * HEADS, REL)

    def exact_dot(left, right, dims):
        high = left.astype(bf16)
        rest = left - high.astype(f32)
        mid = rest.astype(bf16)
        low = (rest - mid.astype(f32)).astype(bf16)
        stacked = jnp.concatenate([high, mid, low], axis=0)
        product = lax.dot_general(stacked, right, dims, preferred_element_type=f32)
        product = product.reshape((3,) + (left.shape[0],) + product.shape[1:])
        return (product[0] + product[1]) + product[2]

    relative = exact_dot(table, hot, (((1,), (1,)), ((), ())))
    relative = relative.reshape(layer_total, HEADS, SLOT, SLOT)
    relative = jnp.concatenate([relative, relative], axis=3)

    region = lax.dynamic_index_in_dim(region_ids, mp_index, 0, keepdims=False)
    rolls = [SHIFT if depth % 2 == 1 else 0 for depth in range(layer_total)]
    perms = {roll: jnp.asarray(permutation(roll)).astype(bf16) for roll in (0, SHIFT)}
    masks = {roll: pair_masks(region, roll) for roll in (0, SHIFT)}

    state = jnp.pad(tokens.astype(f32), ((0, ROWS - count), (0, 0)))
    records = []
    for depth in range(layer_total):
        roll = rolls[depth]
        bias = jnp.concatenate(
            [qv_all[:, depth, 0], jnp.zeros((2, HALF), f32), qv_all[:, depth, 1]], axis=1
        )
        operands = (
            state, perms[roll], weights, norm_gains[depth], norm_biases[depth], bias,
            relative[depth], masks[roll], proj_bias[depth][None], up_all[:, depth],
            fc2_bias[depth][None],
        )
        outs = (
            ((ROWS, WIDTH), f32), ((ROWS, WIDTH), f32), ((ROWS, WIDTH), f32),
            ((2, ROWS, QKV), bf16), ((2, ROWS, HALF), bf16),
            ((2, ROWS, HID), f32), ((2, ROWS, HID), bf16),
        )
        state, *saved = call_kernel(forward_kernel, depth, operands, outs, [], 2_000_000_000)
        records.append(saved)
    block_out = state[:count].astype(bf16)

    gradient = jnp.pad(out_grad.astype(f32), ((0, ROWS - count), (0, 0)))
    wide = None
    small_rows = [None] * layer_total
    for depth in reversed(range(layer_total)):
        roll = rolls[depth]
        operands = (
            gradient, perms[roll], weights, norm_gains[depth], norm_biases[depth],
            relative[depth], masks[roll], *records[depth],
        )
        outs = (
            ((ROWS, WIDTH), f32), ((16, 2, 32, layer_total * COLS), bf16), ((2, WIDTH), f32), ((2, WIDTH), f32),
            ((2, QKV), f32), ((1, WIDTH), f32), ((2, HID), f32), ((1, WIDTH), f32),
            ((HEADS, 128, 128), f32),
        )
        scratch = [pltpu.VMEM((2, ROWS, HALF), bf16), pltpu.VMEM((2, ROWS, QKV), bf16)]
        gradient, wide, *rest = call_kernel(
            backward_kernel, depth, operands, outs, scratch, 4_000_000_000, 1, wide
        )
        gain_sum, off_sum, qkvb_sum, projb_sum, upb_sum, downb_sum, rel_sum = rest
        pairs = rel_sum[:, :SLOT, :SLOT] + rel_sum[:, SLOT:, SLOT:]
        qv_sum = jnp.stack([qkvb_sum[:, :HALF], qkvb_sum[:, 2 * HALF :]]).reshape(-1)
        small_rows[depth] = (gain_sum, off_sum, qv_sum, projb_sum, upb_sum, downb_sum, pairs)

    if n_dp != 16:
        wide = wide.transpose(1, 0, 2, 3).reshape(2, n_dp, shard_rows, layer_total * COLS)
        wide = wide.transpose(1, 0, 2, 3)
    wide = wide.reshape(devices * shard_rows, layer_total * COLS)
    owned = lax.psum_scatter(wide, both, scatter_dimension=0, tiled=True).astype(f32)

    pairs = jnp.concatenate([row[6].reshape(HEADS, -1) for row in small_rows], axis=0)
    table_sum = exact_dot(pairs, hot, (((1,), (0,)), ((), ())))
    member = jnp.concatenate(
        [jnp.concatenate([piece.reshape(-1) for piece in row[:6]]) for row in small_rows]
        + [table_sum.reshape(-1)]
    )
    extent = member.size
    padded = -(-extent // (devices * 128)) * devices * 128
    member = jnp.pad(member, (0, padded - extent)).reshape(devices, padded // devices)
    own = jnp.sum(lax.all_to_all(member, both, 0, 0), axis=0)
    summed = lax.all_gather(own, both, axis=0, tiled=True)
    each = (extent - table_sum.size) // layer_total
    rows = summed[: each * layer_total].reshape(layer_total, each)
    sizes = (2 * WIDTH, 2 * WIDTH, 4 * HALF, WIDTH, 2 * HID, WIDTH)
    edges = np.concatenate([[0], np.cumsum(sizes)])
    gain_t, off_t, qv_t, projb_t, upb_t, downb_t = [
        rows[:, edges[k] : edges[k + 1]] for k in range(6)
    ]
    table_t = summed[each * layer_total : extent].reshape(layer_total, 2, HEADS // 2, REL)
    pick = lambda array, axis: lax.dynamic_index_in_dim(array, mp_index, axis, keepdims=False)
    stacked = owned.reshape(shard_rows, layer_total, COLS).transpose(1, 0, 2)
    ends = np.concatenate([[0], np.cumsum((QKV, HALF, HID, HID))])
    qkv_t, proj_t, up_t, down_t = [stacked[:, :, ends[k] : ends[k + 1]] for k in range(4)]
    return (
        block_out,
        gradient[:count].astype(bf16),
        gain_t.reshape(layer_total, 2, WIDTH),
        off_t.reshape(layer_total, 2, WIDTH),
        qkv_t.reshape(layer_total, shard_rows, 3, HALF),
        pick(qv_t.reshape(layer_total, 2, 2, HALF), 2),
        pick(table_t, 1).transpose(0, 2, 1),
        proj_t.transpose(0, 2, 1),
        projb_t,
        up_t,
        pick(upb_t.reshape(layer_total, 2, HID), 1),
        down_t.transpose(0, 2, 1),
        downb_t,
    )


def solution(mesh):
    in_specs = (
        P(("dp", "mp"), None),
        P("dp", None, None),
        P(),
        P(),
        P(None, "dp", None, "mp"),
        P(None, None, "mp"),
        P(None, None, "mp"),
        P(None, "mp", "dp"),
        P(),
        P(None, "dp", "mp"),
        P(None, "mp"),
        P(None, "mp", "dp"),
        P(),
        P(("dp", "mp"), None),
    )
    out_specs = (
        P(("dp", "mp"), None),
        P(("dp", "mp"), None),
        P(),
        P(),
        P(None, "dp", None, "mp"),
        P(None, None, "mp"),
        P(None, None, "mp"),
        P(None, "mp", "dp"),
        P(),
        P(None, "dp", "mp"),
        P(None, "mp"),
        P(None, "mp", "dp"),
        P(),
    )
    return jax.shard_map(
        per_device, mesh=mesh, in_specs=in_specs, out_specs=out_specs, check_vma=False
    )
```
